32 devices in a mesh: dp: 4 (over y, x), mp: 8 (over z, core).
Axes of the slice: x: 2, y: 2, z: 4, core: 2. Of those that a mesh axis runs over, the one named last changes fastest.
Arguments:
- emb_grad: bfloat16 [76032, 3584], P('mp', 'dp'), may hold values from -70 to 70
- emb_mom: bfloat16 [8, 4, 4, 2376, 896], P('mp', None, 'dp'), may hold values from -0.29882812 to 0.29882812
- blk_grad: bfloat16 [2, 3584, 18944], P(None, 'dp', 'mp'), may hold values from -70 to 70
- blk_mom: bfloat16 [2, 8, 3584, 2368], P(None, None, ('dp', 'mp')), may hold values from -0.29882812 to 0.29882812
- tile_group: int32 [2, 8, 8], replicated, may hold values from 1 to 3
- clip_rms: float32 [4], replicated, may hold values from 0.05 to 80
Outputs:
- emb_update: bfloat16 [8, 4, 4, 2376, 896], P('mp', None, 'dp')
- emb_moment: bfloat16 [8, 4, 4, 2376, 896], P('mp', None, 'dp')
- blk_update: bfloat16 [2, 8, 3584, 2368], P(None, None, ('dp', 'mp'))
- blk_moment: bfloat16 [2, 8, 3584, 2368], P(None, None, ('dp', 'mp'))
The draws below stay inside these ranges and needn't reach their ends.
All inputs are finite; a program needn't handle non-finite values.
Results may differ from the reference program's by a relative error of at most 0.001.
Values may be sent and summed in bfloat16 or wider, within the bound.
A program may use at most 192 MiB of HBM per device.

```python
import math
import jax
import jax.numpy as jnp
from jax import lax

D = 3584
FF = 18944
V = 76032
G = 4
RB = 2
ID_ROWS = 8
EMB_OWN = 2376
DC = 896
FFC = 2368
N_DP = 4
N_MP = 8


def rough_scales(key, count, top):
    return jnp.exp(jax.random.uniform(key, (count,), jnp.float32) * math.log(top))


def block_scales(key, blocks, width, top):
    place = jnp.arange(blocks, dtype=jnp.float32) / float(max(blocks - 1, 1))
    unit = jax.random.uniform(key, (blocks,), jnp.float32)
    scales = jnp.exp((0.5 * place + 0.5 * unit) * math.log(top))
    return jnp.repeat(scales, width, total_repeat_length=blocks * width)


def draw_emb_grad(key, part):
    first_key = jax.random.fold_in(key, 0)
    second_key = jax.random.fold_in(key, 1)
    fourth_key = jax.random.fold_in(key, 3)
    fifth_key = jax.random.fold_in(key, 4)
    column_blocks = D // DC
    row_blocks = V // (EMB_OWN * column_blocks)
    rowscale = rough_scales(second_key, V, 10.0) * block_scales(fourth_key, row_blocks, V // row_blocks, 10.0)
    colscale = block_scales(fifth_key, column_blocks, DC, 3.0)
    values = jnp.clip(jax.random.normal(first_key, (V, D), jnp.float32), -4.0, 4.0) * 0.058
    values = values * rowscale[:, None] * colscale[None, :]
    return values.astype(jnp.bfloat16)


def draw_blk_grad(key, part):
    first_key = jax.random.fold_in(jax.random.fold_in(key, 7), 0)
    second_key = jax.random.fold_in(jax.random.fold_in(key, 7), 1)
    fourth_key = jax.random.fold_in(jax.random.fold_in(key, 7), 3)
    fifth_key = jax.random.fold_in(jax.random.fold_in(key, 7), 4)
    row_blocks = D // DC
    column_blocks = FF // FFC
    rowscale = rough_scales(second_key, D, 10.0) * block_scales(fourth_key, row_blocks, DC, 3.0)
    colscale = block_scales(fifth_key, column_blocks, FFC, 10.0)
    values = jnp.clip(jax.random.normal(first_key, (2, D, FF), jnp.float32), -4.0, 4.0) * 0.058
    values = values * rowscale[None, :, None] * colscale[None, None, :]
    return values.astype(jnp.bfloat16)


def draw_clip_rms(key, part):
    first_key, second_key = jax.random.split(jax.random.fold_in(key, 11))
    order = jax.random.permutation(first_key, G)
    lower = order < G // 2
    unit = jax.random.uniform(second_key, (G,), jnp.float32)
    small_values = 0.05 * jnp.exp(unit * math.log(10.0))
    large_values = 40.0 * jnp.exp(unit * math.log(2.0))
    return jnp.where(lower, small_values, large_values).astype(jnp.float32)


def set_ends(entries, stream_key, low, high):
    spot = [jax.random.randint(jax.random.fold_in(stream_key, axis), (), 0, length) for axis, length in enumerate(entries.shape)]
    longest = entries.shape.index(max(entries.shape))
    neighbour = spot[:longest] + [(spot[longest] + 1) % entries.shape[longest]] + spot[longest + 1:]
    return entries.at[tuple(spot)].set(low).at[tuple(neighbour)].set(high)


def block_scale(stream_key, dims, cuts, least, largest):
    def one(position, shards_of):
        steps = jax.random.uniform(jax.random.fold_in(jax.random.fold_in(stream_key, 6), position), (shards_of,), jnp.float32, least / len(cuts), largest / len(cuts))
        return jnp.repeat(jnp.exp(steps), dims[position] // shards_of).reshape((-1,) + (1,) * (len(dims) - position - 1))

    loudness = one(*cuts[0])
    for cut in cuts[1:]:
        loudness = loudness * one(*cut)
    return loudness


def noise(rng, extent, spread, most, cuts=(), kind=jnp.bfloat16):
    factor_of = block_scale(rng, extent, cuts, -0.22, 0.18) if cuts else 1.0
    values = jax.random.normal(rng, extent, jnp.float32) * spread * factor_of
    return jnp.minimum(jnp.maximum(values, -most), most).astype(kind)


def setup_inputs(seed: int = 0) -> dict:
    streams_of = jax.random.split(jax.random.key(seed), 7)
    emb_grad = draw_emb_grad(jax.random.fold_in(streams_of[6], 71), 0)
    emb_mom = noise(streams_of[1], (N_MP, N_DP, N_DP, EMB_OWN, DC), 0.05, 0.29882812, ((0, 8), (2, 4)))
    blk_grad = draw_blk_grad(jax.random.fold_in(streams_of[6], 71), 0)
    blk_mom = noise(streams_of[3], (2, N_MP, D, FFC), 0.05, 0.29882812, ((2, 32),))
    tile_group = set_ends(jax.random.randint(streams_of[4], (2, ID_ROWS, N_MP), 1, G), jax.random.fold_in(streams_of[4], 1), 1, G - 1).astype(jnp.int32)
    clip_rms = draw_clip_rms(jax.random.fold_in(streams_of[6], 71), 0)
    return {"emb_grad": emb_grad, "emb_mom": emb_mom, "blk_grad": blk_grad, "blk_mom": blk_mom, "tile_group": tile_group, "clip_rms": clip_rms}


beta_first = 0.9
beta_second = 0.99
temper = 0.05
epsilon = 1e-06

def lion_step(clipped, moment):
    moment = moment.astype(jnp.float32)
    update = jnp.tanh((beta_first * moment + (1.0 - beta_first) * clipped) / temper).astype(jnp.bfloat16)
    new_moment = (beta_second * moment + (1.0 - beta_second) * clipped).astype(jnp.bfloat16)
    return (update, new_moment)

def square_sum(pieces):
    return jnp.sum(jnp.square(pieces.astype(jnp.float32)))

def reference(emb_grad, emb_mom, blk_grad, blk_mom, tile_group, clip_rms):
    block_height = D // (RB * N_DP)
    block_cols = FF // N_MP
    labels = jnp.arange(G, dtype=jnp.int32)
    first = (labels == 0).astype(jnp.float32)
    onehot = (tile_group[..., None] == labels).astype(jnp.float32)
    spans = emb_grad.reshape(N_MP * N_DP, EMB_OWN, D)
    emb_squares = jnp.sum(lax.map(square_sum, spans))
    block = blk_grad.astype(jnp.float32).reshape(2, RB * N_DP, block_height, N_MP, block_cols)
    block_squares = lax.optimization_barrier(jnp.sum(jnp.square(block), axis=(2, 4)))
    totals = lax.optimization_barrier(jnp.sum(block_squares[..., None] * onehot, axis=(0, 1, 2))) + emb_squares * first
    counts = lax.optimization_barrier(jnp.sum(onehot, axis=(0, 1, 2))) * float(block_height * block_cols) + first * float(V * D)
    root_mean = jnp.sqrt(totals / jnp.maximum(counts, 1.0))
    factor = jnp.minimum(1.0, clip_rms / (root_mean + epsilon))
    moments = jnp.transpose(emb_mom, (0, 2, 3, 1, 4)).reshape(N_MP * N_DP, EMB_OWN, D)

    def embed_span(paired):
        return lion_step(paired[0].astype(jnp.float32) * factor[0], paired[1])
    emb_update, emb_moment = lax.map(embed_span, (spans, moments))

    def to_owner(values):
        return jnp.transpose(values.reshape(N_MP, N_DP, EMB_OWN, N_DP, D // N_DP), (0, 3, 1, 2, 4))
    block_factor = lax.optimization_barrier(jnp.sum(onehot * factor, axis=-1))
    clipped = (block * block_factor[:, :, None, :, None]).reshape(2, D, N_MP, block_cols)
    blk_plain = jnp.transpose(blk_mom, (0, 2, 1, 3))
    blk_update, blk_moment = lion_step(clipped, blk_plain)
    return (to_owner(emb_update), to_owner(emb_moment), jnp.transpose(blk_update, (0, 2, 1, 3)), jnp.transpose(blk_moment, (0, 2, 1, 3)))
```

```python
import functools

import jax
import jax.numpy as jnp
from jax import lax
from jax.experimental import pallas as pl
from jax.experimental.pallas import tpu as pltpu
from jax.sharding import PartitionSpec as P

beta_first = 0.9
beta_second = 0.99
temper = 0.05
epsilon = 1e-06
vmem_bytes = 40 * 1024 * 1024


def partner_tables(count):
    if count & (count - 1) == 0:
        return (lambda i, k: i ^ k), (lambda i, k: i ^ k)
    return (lambda i, k: (i + k) % count), (lambda i, k: (i + count - k) % count)


def lion_block(grad, moment, factor):
    grad = grad.astype(jnp.float32)
    moment = moment.astype(jnp.float32)
    update = jnp.tanh(
        moment * (beta_first / temper) + grad * (factor * ((1.0 - beta_first) / temper))
    )
    new_moment = moment * beta_second + grad * (factor * (1.0 - beta_second))
    return update.astype(jnp.bfloat16), new_moment.astype(jnp.bfloat16)


def emb_body(count, aliased, sources, factors, *refs):
    pieces = refs[:count]
    moment = refs[count]
    update_out, moment_out = refs[count + 1 + aliased :]
    k = pl.program_id(0)
    for j in range(count):

        @pl.when(k == j)
        def _():
            update, new_moment = lion_block(pieces[j][...].reshape(moment.shape), moment[...], factors[0])
            update_out[...] = update
            moment_out[...] = new_moment


def emb_step(sources, factors, own, pieces, mom, start, rows, block, outs):
    count = mom.shape[0]
    features = mom.shape[2]
    blocks = pl.cdiv(rows, block)
    first = start // block

    def piece_map(j):
        def index(k, r, s, f):
            return (jnp.where(k < j, 0, jnp.where(k > j, blocks - 1, r)), 0)

        return index

    def own_map(k, r, s, f):
        return (s[0], first + jnp.where(k > 0, blocks - 1, r), 0)

    def mom_map(k, r, s, f):
        return (s[k], first + r, 0)

    whole = pl.BlockSpec((1, block, features), mom_map)
    in_specs = (
        [pl.BlockSpec((1, block, features), own_map)]
        + [pl.BlockSpec((block, features), piece_map(j)) for j in range(1, count)]
        + [whole]
        + [pl.BlockSpec(memory_space=pl.ANY)] * len(outs)
    )
    shape = jax.ShapeDtypeStruct(mom.shape, jnp.bfloat16)
    base = 2 + count + 1
    size = count * rows * features
    return pl.pallas_call(
        functools.partial(emb_body, count, len(outs)),
        out_shape=(shape, shape),
        grid_spec=pltpu.PrefetchScalarGridSpec(
            num_scalar_prefetch=2,
            grid=(count, blocks),
            in_specs=in_specs,
            out_specs=[whole, whole],
        ),
        input_output_aliases={base + i: i for i in range(len(outs))},
        compiler_params=pltpu.CompilerParams(vmem_limit_bytes=vmem_bytes),
        cost_estimate=pl.CostEstimate(flops=8 * size, bytes_accessed=8 * size, transcendentals=size),
    )(sources, factors, own, *pieces, mom, *outs)


def blk_body(count, matrix, aliased, sources, factors, *refs):
    pieces = refs[:count]
    moment = refs[count]
    update_out, moment_out = refs[count + 1 + aliased :]
    k = pl.program_id(0)
    factor = factors[matrix, sources[k]]
    for j in range(count):

        @pl.when(k == j)
        def _():
            update, new_moment = lion_block(pieces[j][...].reshape(moment.shape), moment[...], factor)
            update_out[...] = update
            moment_out[...] = new_moment


def blk_step(sources, factors, pieces, mom, matrix, outs):
    count = mom.shape[1]
    rows, columns = mom.shape[2:]
    whole = pl.BlockSpec((1, 1, rows, columns), lambda k, s, f: (matrix, s[k], 0, 0))
    in_specs = (
        [pl.BlockSpec((rows, columns), lambda k, s, f: (0, 0))] * count
        + [whole]
        + [pl.BlockSpec(memory_space=pl.ANY)] * len(outs)
    )
    shape = jax.ShapeDtypeStruct(mom.shape, jnp.bfloat16)
    base = 2 + count + 1
    size = count * rows * columns
    return pl.pallas_call(
        functools.partial(blk_body, count, matrix, len(outs)),
        out_shape=(shape, shape),
        grid_spec=pltpu.PrefetchScalarGridSpec(
            num_scalar_prefetch=2,
            grid=(count,),
            in_specs=in_specs,
            out_specs=[whole, whole],
        ),
        input_output_aliases={base + i: i for i in range(len(outs))},
        compiler_params=pltpu.CompilerParams(vmem_limit_bytes=vmem_bytes),
        cost_estimate=pl.CostEstimate(flops=8 * size, bytes_accessed=8 * size, transcendentals=size),
    )(sources, factors, *pieces, mom, *outs)


def on_device(emb_grad, emb_mom, blk_grad, blk_mom, tile_group, clip_rms):
    dp_count = lax.axis_size("dp")
    mp_count = lax.axis_size("mp")
    dp_index = lax.axis_index("dp")
    mp_index = lax.axis_index("mp")
    groups = clip_rms.shape[0]
    tile_rows, tile_cols = emb_grad.shape
    own_rows = emb_mom.shape[3]
    feature_block = emb_mom.shape[4]
    matrices, block_rows, block_cols = blk_grad.shape
    owner_rows = blk_mom.shape[2]
    row_blocks = tile_group.shape[1] // dp_count
    block_height = block_rows // row_blocks
    labels = jnp.arange(groups, dtype=jnp.int32)
    first = (labels == 0).astype(jnp.float32)
    onehot = (tile_group[..., None] == labels).astype(jnp.float32)
    counts = jnp.sum(onehot, axis=(0, 1, 2)) * float(block_height * block_cols) + first * float(
        tile_rows * mp_count * tile_cols * dp_count
    )
    owner_block = dp_index * row_blocks + mp_index * owner_rows // block_height
    owner_ids = lax.dynamic_index_in_dim(onehot, owner_block, axis=1, keepdims=False)

    emb_to, emb_from = partner_tables(dp_count)
    blk_to, blk_from = partner_tables(mp_count)
    emb_pieces = emb_grad.reshape(dp_count, own_rows, feature_block)
    mom_local = emb_mom.reshape(dp_count, own_rows, feature_block)
    block = 256 if own_rows > 1024 else 128
    cut = (own_rows * 3 // 4) // block * block
    spans = ((0, cut), (cut, own_rows - cut))

    def emb_send(start, rows, tie=None):
        got = []
        for k in range(1, dp_count):
            piece = lax.dynamic_slice(
                emb_pieces, (emb_to(dp_index, k), start, 0), (1, rows, feature_block)
            )[0]
            if tie is not None:
                piece, _ = lax.optimization_barrier((piece, tie[k - 1]))
            pairs = [(i, emb_to(i, k)) for i in range(dp_count)]
            got.append(lax.ppermute(piece, "dp", pairs))
        return got

    blk_pieces = blk_grad.reshape(matrices, mp_count, owner_rows, block_cols)

    def blk_send(matrix, tie=None):
        got = []
        for k in range(mp_count):
            piece = lax.dynamic_index_in_dim(blk_pieces[matrix], blk_to(mp_index, k), axis=0, keepdims=False)
            if k > 0:
                if tie is not None:
                    piece, _ = lax.optimization_barrier((piece, tie[k]))
                pairs = [(i, blk_to(i, k)) for i in range(mp_count)]
                piece = lax.ppermute(piece, "mp", pairs)
            got.append(piece)
        return got

    emb_got = [emb_send(*spans[0])]
    blk_got = [blk_send(0)]
    emb_got.append(emb_send(*spans[1], tie=emb_got[0]))
    for matrix in range(1, matrices):
        blk_got.append(blk_send(matrix, tie=blk_got[-1]))

    emb_squares = jnp.sum(jnp.square(emb_grad.astype(jnp.float32)))
    block_squares = jnp.sum(
        jnp.square(blk_grad.astype(jnp.float32)).reshape(
            matrices, row_blocks, block_height, block_cols
        ),
        axis=(2, 3),
    )
    tile_rows_ids = lax.dynamic_slice_in_dim(onehot, dp_index * row_blocks, row_blocks, axis=1)
    tile_ids = lax.dynamic_index_in_dim(tile_rows_ids, mp_index, axis=2, keepdims=False)
    block_terms = jnp.sum(block_squares[..., None] * tile_ids, axis=(0, 1))
    partial_value = block_terms + emb_squares * first
    totals = lax.psum(partial_value, ("dp", "mp"))
    root_mean = jnp.sqrt(totals / jnp.maximum(counts, 1.0))
    factor = jnp.minimum(1.0, clip_rms / (root_mean + epsilon))
    owner_factor = jnp.sum(owner_ids * factor, axis=-1)

    emb_sources = jnp.stack([emb_from(dp_index, k) for k in range(dp_count)]).astype(jnp.int32)
    blk_sources = jnp.stack([blk_from(mp_index, k) for k in range(mp_count)]).astype(jnp.int32)
    emb_outs = ()
    for (start, rows), got in zip(spans, emb_got):
        emb_outs = emb_step(
            emb_sources, factor, emb_pieces, got, mom_local, start, rows, block, emb_outs
        )
    blk_outs = ()
    for matrix in range(matrices):
        blk_outs = blk_step(blk_sources, owner_factor, blk_got[matrix], blk_mom, matrix, blk_outs)
    return (
        emb_outs[0].reshape(emb_mom.shape),
        emb_outs[1].reshape(emb_mom.shape),
        blk_outs[0],
        blk_outs[1],
    )


def solution(mesh):
    placed = (
        P("mp", "dp"),
        P("mp", None, "dp", None, None),
        P(None, "dp", "mp"),
        P(None, None, ("dp", "mp"), None),
        P(),
        P(),
    )
    return jax.shard_map(
        on_device,
        mesh=mesh,
        in_specs=placed,
        out_specs=(
            P("mp", None, "dp", None, None),
            P("mp", None, "dp", None, None),
            P(None, None, ("dp", "mp"), None),
            P(None, None, ("dp", "mp"), None),
        ),
        check_vma=False,
    )
```

```python
import functools

import jax
import jax.numpy as jnp
from jax import lax
from jax.experimental import pallas as pl
from jax.experimental.pallas import tpu as pltpu
from jax.sharding import PartitionSpec as P

beta_first = 0.9
beta_second = 0.99
temper = 0.05
epsilon = 1e-06
vmem_bytes = 60 * 1024 * 1024


def partner_tables(count):
    if count & (count - 1) == 0:
        return (lambda i, k: i ^ k), (lambda i, k: i ^ k)
    return (lambda i, k: (i + k) % count), (lambda i, k: (i + count - k) % count)


def lion_rows(grad, moment, factor):
    grad = grad.astype(jnp.float32)
    moment = moment.astype(jnp.float32)
    update = jnp.tanh(
        moment * (beta_first / temper) + grad * (factor * ((1.0 - beta_first) / temper))
    )
    new_moment = moment * beta_second + grad * (factor * (1.0 - beta_second))
    return update.astype(jnp.bfloat16), new_moment.astype(jnp.bfloat16)


def lion_block(grad, moment, update_out, moment_out, factor):
    rows = moment.shape[0]
    height = 16 if rows > 128 and rows % 16 == 0 else rows

    @pl.loop(0, rows // height)
    def _(i):
        at = pl.ds(pl.multiple_of(i * height, height), height)
        update, new_moment = lion_rows(grad[at, :], moment[at, :], factor)
        update_out[at, :] = update
        moment_out[at, :] = new_moment


def emb_body(count, sources, factors, *refs):
    own, *pieces = refs[:count]
    pieces = [own.at[0]] + pieces
    moment, update_out, moment_out = refs[count:]
    k = pl.program_id(0)
    for j in range(count):

        @pl.when(k == j)
        def _():
            lion_block(pieces[j], moment.at[0], update_out.at[0], moment_out.at[0], factors[0])


def emb_step(sources, factors, own, pieces, mom, block):
    count, rows, features = mom.shape
    blocks = pl.cdiv(rows, block)

    def piece_map(j):
        def index(k, r, s, f):
            return (jnp.where(k < j, 0, jnp.where(k > j, blocks - 1, r)), 0)

        return index

    def own_map(k, r, s, f):
        return (s[0], jnp.where(k > 0, blocks - 1, r), 0)

    def mom_map(k, r, s, f):
        return (s[k], r, 0)

    whole = pl.BlockSpec((1, block, features), mom_map)
    in_specs = (
        [pl.BlockSpec((1, block, features), own_map)]
        + [pl.BlockSpec((block, features), piece_map(j)) for j in range(1, count)]
        + [whole]
    )
    shape = jax.ShapeDtypeStruct(mom.shape, jnp.bfloat16)
    size = count * rows * features
    return pl.pallas_call(
        functools.partial(emb_body, count),
        out_shape=(shape, shape),
        grid_spec=pltpu.PrefetchScalarGridSpec(
            num_scalar_prefetch=2,
            grid=(count, blocks),
            in_specs=in_specs,
            out_specs=[whole, whole],
        ),
        compiler_params=pltpu.CompilerParams(vmem_limit_bytes=vmem_bytes),
        cost_estimate=pl.CostEstimate(flops=8 * size, bytes_accessed=8 * size, transcendentals=size),
    )(sources, factors, own, *pieces, mom)


def blk_body(factors, grad, moment, update_out, moment_out):
    factor = factors[pl.program_id(0), pl.program_id(1)]
    lion_block(
        grad.at[0, 0], moment.at[0, 0], update_out.at[0, 0], moment_out.at[0, 0], factor
    )


def blk_step(factors, grad, mom):
    matrices, count, rows, columns = mom.shape
    block = (1, 1, rows, columns)
    whole = pl.BlockSpec(block, lambda m, c, f: (m, c, 0, 0))
    shape = jax.ShapeDtypeStruct(mom.shape, jnp.bfloat16)
    return pl.pallas_call(
        blk_body,
        out_shape=(shape, shape),
        grid_spec=pltpu.PrefetchScalarGridSpec(
            num_scalar_prefetch=1,
            grid=(matrices, count),
            in_specs=[pl.BlockSpec(block, lambda m, c, f: (c, m, 0, 0)), whole],
            out_specs=[whole, whole],
        ),
        compiler_params=pltpu.CompilerParams(vmem_limit_bytes=vmem_bytes),
        cost_estimate=pl.CostEstimate(
            flops=8 * mom.size, bytes_accessed=8 * mom.size, transcendentals=mom.size
        ),
    )(factors, grad, mom)


def on_device(emb_grad, emb_mom, blk_grad, blk_mom, tile_group, clip_rms):
    dp_count = lax.axis_size("dp")
    mp_count = lax.axis_size("mp")
    dp_index = lax.axis_index("dp")
    mp_index = lax.axis_index("mp")
    groups = clip_rms.shape[0]
    tile_rows, tile_cols = emb_grad.shape
    own_rows = emb_mom.shape[3]
    feature_block = emb_mom.shape[4]
    matrices, block_rows, block_cols = blk_grad.shape
    owner_rows = blk_mom.shape[2]
    row_blocks = tile_group.shape[1] // dp_count
    block_height = block_rows // row_blocks
    labels = jnp.arange(groups, dtype=jnp.int32)
    first = (labels == 0).astype(jnp.float32)
    onehot = (tile_group[..., None] == labels).astype(jnp.float32)
    counts = jnp.sum(onehot, axis=(0, 1, 2)) * float(block_height * block_cols) + first * float(
        tile_rows * mp_count * tile_cols * dp_count
    )
    owner_block = dp_index * row_blocks + mp_index * owner_rows // block_height
    owner_ids = lax.dynamic_index_in_dim(onehot, owner_block, axis=1, keepdims=False)

    emb_to, emb_from = partner_tables(dp_count)
    emb_pieces = emb_grad.reshape(dp_count, own_rows, feature_block)
    mom_local = emb_mom.reshape(dp_count, own_rows, feature_block)
    emb_got = []
    for k in range(1, dp_count):
        piece = lax.dynamic_index_in_dim(emb_pieces, emb_to(dp_index, k), axis=0, keepdims=False)
        emb_got.append(lax.ppermute(piece, "dp", [(i, emb_to(i, k)) for i in range(dp_count)]))
    blk_pieces = jnp.swapaxes(
        blk_grad.reshape(matrices, mp_count, owner_rows, block_cols), 0, 1
    )
    blk_owner = lax.all_to_all(blk_pieces, "mp", split_axis=0, concat_axis=0, tiled=True)

    emb_squares = jnp.sum(jnp.square(emb_grad.astype(jnp.float32)))
    block_squares = jnp.sum(
        jnp.square(blk_grad.astype(jnp.float32)).reshape(
            matrices, row_blocks, block_height, block_cols
        ),
        axis=(2, 3),
    )
    tile_rows_ids = lax.dynamic_slice_in_dim(onehot, dp_index * row_blocks, row_blocks, axis=1)
    tile_ids = lax.dynamic_index_in_dim(tile_rows_ids, mp_index, axis=2, keepdims=False)
    block_terms = jnp.sum(block_squares[..., None] * tile_ids, axis=(0, 1))
    partial_value = block_terms + emb_squares * first
    totals = lax.psum(partial_value, ("dp", "mp"))
    root_mean = jnp.sqrt(totals / jnp.maximum(counts, 1.0))
    factor = jnp.minimum(1.0, clip_rms / (root_mean + epsilon))
    owner_factor = jnp.sum(owner_ids * factor, axis=-1)

    emb_sources = jnp.stack([emb_from(dp_index, k) for k in range(dp_count)]).astype(jnp.int32)
    block = pl.cdiv(pl.cdiv(own_rows, 3), 16) * 16
    blk_outs = blk_step(owner_factor, blk_owner, blk_mom)
    emb_outs = emb_step(emb_sources, factor, emb_pieces, emb_got, mom_local, block)
    return (
        emb_outs[0].reshape(emb_mom.shape),
        emb_outs[1].reshape(emb_mom.shape),
        blk_outs[0],
        blk_outs[1],
    )


def solution(mesh):
    placed = (
        P("mp", "dp"),
        P("mp", None, "dp", None, None),
        P(None, "dp", "mp"),
        P(None, None, ("dp", "mp"), None),
        P(),
        P(),
    )
    return jax.shard_map(
        on_device,
        mesh=mesh,
        in_specs=placed,
        out_specs=(
            P("mp", None, "dp", None, None),
            P("mp", None, "dp", None, None),
            P(None, None, ("dp", "mp"), None),
            P(None, None, ("dp", "mp"), None),
        ),
        check_vma=False,
    )
```

```python
import functools

import jax
import jax.numpy as jnp
from jax import lax
from jax.experimental import pallas as pl
from jax.experimental.pallas import tpu as pltpu
from jax.sharding import PartitionSpec as P

beta_first = 0.9
beta_second = 0.99
temper = 0.05
epsilon = 1e-06
vmem_bytes = 60 * 1024 * 1024


def partner_tables(count):
    if count & (count - 1) == 0:
        return (lambda i, k: i ^ k), (lambda i, k: i ^ k)
    return (lambda i, k: (i + k) % count), (lambda i, k: (i + count - k) % count)


def lion_rows(grad, moment, factor):
    grad = grad.astype(jnp.float32)
    moment = moment.astype(jnp.float32)
    update = jnp.tanh(
        moment * (beta_first / temper) + grad * (factor * ((1.0 - beta_first) / temper))
    )
    new_moment = moment * beta_second + grad * (factor * (1.0 - beta_second))
    return update.astype(jnp.bfloat16), new_moment.astype(jnp.bfloat16)


def lion_block(grad, moment, update_out, moment_out, factor):
    rows = moment.shape[0]
    height = 16 if rows > 128 and rows % 16 == 0 else rows

    @pl.loop(0, rows // height)
    def _(i):
        at = pl.ds(pl.multiple_of(i * height, height), height)
        update, new_moment = lion_rows(grad[at, :], moment[at, :], factor)
        update_out[at, :] = update
        moment_out[at, :] = new_moment


def emb_body(count, sources, factors, *refs):
    own, *pieces = refs[:count]
    pieces = [own.at[0]] + pieces
    moment, update_out, moment_out = refs[count:]
    k = pl.program_id(0)
    for j in range(count):

        @pl.when(k == j)
        def _():
            lion_block(pieces[j], moment.at[0], update_out.at[0], moment_out.at[0], factors[0])


def emb_step(sources, factors, own, pieces, mom, block):
    count, rows, features = mom.shape
    blocks = pl.cdiv(rows, block)

    def piece_map(j):
        def index(k, r, s, f):
            return (jnp.where(k < j, 0, jnp.where(k > j, blocks - 1, r)), 0)

        return index

    def own_map(k, r, s, f):
        return (s[0], jnp.where(k > 0, blocks - 1, r), 0)

    def mom_map(k, r, s, f):
        return (s[k], r, 0)

    whole = pl.BlockSpec((1, block, features), mom_map)
    in_specs = (
        [pl.BlockSpec((1, block, features), own_map)]
        + [pl.BlockSpec((block, features), piece_map(j)) for j in range(1, count)]
        + [whole]
    )
    shape = jax.ShapeDtypeStruct(mom.shape, jnp.bfloat16)
    size = count * rows * features
    return pl.pallas_call(
        functools.partial(emb_body, count),
        out_shape=(shape, shape),
        grid_spec=pltpu.PrefetchScalarGridSpec(
            num_scalar_prefetch=2,
            grid=(count, blocks),
            in_specs=in_specs,
            out_specs=[whole, whole],
        ),
        compiler_params=pltpu.CompilerParams(vmem_limit_bytes=vmem_bytes),
        cost_estimate=pl.CostEstimate(flops=8 * size, bytes_accessed=8 * size, transcendentals=size),
    )(sources, factors, own, *pieces, mom)


def blk_body(factors, grad, moment, update_out, moment_out):
    factor = factors[pl.program_id(0), pl.program_id(1)]
    lion_block(
        grad.at[0, 0], moment.at[0, 0], update_out.at[0, 0], moment_out.at[0, 0], factor
    )


def blk_step(factors, grad, mom):
    matrices, count, rows, columns = mom.shape
    block = (1, 1, rows, columns)
    whole = pl.BlockSpec(block, lambda m, c, f: (m, c, 0, 0))
    shape = jax.ShapeDtypeStruct(mom.shape, jnp.bfloat16)
    return pl.pallas_call(
        blk_body,
        out_shape=(shape, shape),
        grid_spec=pltpu.PrefetchScalarGridSpec(
            num_scalar_prefetch=1,
            grid=(matrices, count),
            in_specs=[pl.BlockSpec(block, lambda m, c, f: (c, m, 0, 0)), whole],
            out_specs=[whole, whole],
        ),
        compiler_params=pltpu.CompilerParams(vmem_limit_bytes=vmem_bytes),
        cost_estimate=pl.CostEstimate(
            flops=8 * mom.size, bytes_accessed=8 * mom.size, transcendentals=mom.size
        ),
    )(factors, grad, mom)


def on_device(emb_grad, emb_mom, blk_grad, blk_mom, tile_group, clip_rms):
    dp_count = lax.axis_size("dp")
    mp_count = lax.axis_size("mp")
    dp_index = lax.axis_index("dp")
    mp_index = lax.axis_index("mp")
    groups = clip_rms.shape[0]
    tile_rows, tile_cols = emb_grad.shape
    own_rows = emb_mom.shape[3]
    feature_block = emb_mom.shape[4]
    matrices, block_rows, block_cols = blk_grad.shape
    owner_rows = blk_mom.shape[2]
    row_blocks = tile_group.shape[1] // dp_count
    block_height = block_rows // row_blocks
    labels = jnp.arange(groups, dtype=jnp.int32)
    first = (labels == 0).astype(jnp.float32)
    onehot = (tile_group[..., None] == labels).astype(jnp.float32)
    counts = jnp.sum(onehot, axis=(0, 1, 2)) * float(block_height * block_cols) + first * float(
        tile_rows * mp_count * tile_cols * dp_count
    )
    owner_block = dp_index * row_blocks + mp_index * owner_rows // block_height
    owner_ids = lax.dynamic_index_in_dim(onehot, owner_block, axis=1, keepdims=False)

    emb_to, emb_from = partner_tables(dp_count)
    emb_pieces = emb_grad.reshape(dp_count, own_rows, feature_block)
    mom_local = emb_mom.reshape(dp_count, own_rows, feature_block)
    emb_got = []
    cut = [
        lax.dynamic_index_in_dim(emb_pieces, emb_to(dp_index, k), axis=0, keepdims=False)
        for k in range(1, dp_count)
    ]
    cut, blk_sent = lax.optimization_barrier((cut, blk_grad))
    for k, piece in enumerate(cut, 1):
        emb_got.append(lax.ppermute(piece, "dp", [(i, emb_to(i, k)) for i in range(dp_count)]))
    blk_pieces = jnp.swapaxes(
        blk_sent.reshape(matrices, mp_count, owner_rows, block_cols), 0, 1
    )
    blk_owner = lax.all_to_all(blk_pieces, "mp", split_axis=0, concat_axis=0, tiled=True)

    emb_squares = jnp.sum(jnp.square(emb_grad.astype(jnp.float32)))
    block_squares = jnp.sum(
        jnp.square(blk_grad.astype(jnp.float32)).reshape(
            matrices, row_blocks, block_height, block_cols
        ),
        axis=(2, 3),
    )
    tile_rows_ids = lax.dynamic_slice_in_dim(onehot, dp_index * row_blocks, row_blocks, axis=1)
    tile_ids = lax.dynamic_index_in_dim(tile_rows_ids, mp_index, axis=2, keepdims=False)
    block_terms = jnp.sum(block_squares[..., None] * tile_ids, axis=(0, 1))
    partial_value = block_terms + emb_squares * first
    totals = lax.psum(partial_value, ("dp", "mp"))
    root_mean = jnp.sqrt(totals / jnp.maximum(counts, 1.0))
    factor = jnp.minimum(1.0, clip_rms / (root_mean + epsilon))
    owner_factor = jnp.sum(owner_ids * factor, axis=-1)

    emb_sources = jnp.stack([emb_from(dp_index, k) for k in range(dp_count)]).astype(jnp.int32)
    block = pl.cdiv(pl.cdiv(own_rows, 3), 16) * 16
    blk_outs = blk_step(owner_factor, blk_owner, blk_mom)
    emb_outs = emb_step(emb_sources, factor, emb_pieces, emb_got, mom_local, block)
    return (
        emb_outs[0].reshape(emb_mom.shape),
        emb_outs[1].reshape(emb_mom.shape),
        blk_outs[0],
        blk_outs[1],
    )


def solution(mesh):
    placed = (
        P("mp", "dp"),
        P("mp", None, "dp", None, None),
        P(None, "dp", "mp"),
        P(None, None, ("dp", "mp"), None),
        P(),
        P(),
    )
    return jax.shard_map(
        on_device,
        mesh=mesh,
        in_specs=placed,
        out_specs=(
            P("mp", None, "dp", None, None),
            P("mp", None, "dp", None, None),
            P(None, None, ("dp", "mp"), None),
            P(None, None, ("dp", "mp"), None),
        ),
        check_vma=False,
    )
```
